256 devices in a mesh: ctx: 32 (over z, x), dp: 8 (over y, core).
Axes of the slice: x: 4, y: 4, z: 8, core: 2. Of those that a mesh axis runs over, the one named last changes fastest.
Arguments:
- queries: bfloat16 [8, 16384, 1024], P('dp', 'ctx'), may hold values from -256 to 256
- keys: bfloat16 [8, 16384, 1024], P('dp', 'ctx'), may hold values from -4 to 4
- values: bfloat16 [8, 16384, 1024], P('dp', 'ctx'), may hold values from -6 to 6
- grad_out: bfloat16 [8, 16384, 1024], P('dp', 'ctx'), may hold values from -6 to 6
- out_weight: bfloat16 [1024, 1024], replicated, may hold values from -0.5 to 0.5
Outputs:
- mixed: bfloat16 [8, 16384, 1024], P('dp', 'ctx')
- grad_queries: bfloat16 [8, 16384, 1024], P('dp', 'ctx')
- grad_keys: bfloat16 [8, 16384, 1024], P('dp', 'ctx')
- grad_values: bfloat16 [8, 16384, 1024], P('dp', 'ctx')
- grad_weight: float32 [1024, 1024], P('ctx')
The draws below stay inside these ranges and needn't reach their ends.
All inputs are finite; a program needn't handle non-finite values.
Results may differ from the reference program's by a relative error of at most 0.025.
Values may be sent and summed in bfloat16 or wider, within the bound.
No kernel may reach another device: no remote copies, remote signals or barrier semaphores. Data moves between devices by JAX's collectives and lax.ppermute only.
A program may use at most 128 MiB of HBM per device.

```python
import math
import jax
import jax.numpy as jnp
from jax import lax

HEADS = 8
HEAD = 128
DMODEL = 1024
BLOCK = 256
POOL = 16
GROUP = 8
TOK_DEV = 512
BATCH = 8
SEQ = 16384
HE = 1024
N_CTX = 32


def shared_rows(key):
    keyset = jax.random.split(key, 1)
    width = HEADS * HEAD
    normal_part = jax.random.truncated_normal(keyset[0], -4.0, 4.0, (BATCH, SEQ, width), jnp.float32)
    base = normal_part
    return base


def draw_keys(key, part):
    root = key
    base = shared_rows(root)
    result = base
    return result.astype(jnp.bfloat16)


def draw_queries(key, part):
    key = jax.random.fold_in(key, 5)
    width = HEADS * HEAD
    result = 2.0 * jax.random.truncated_normal(key, -4.0, 4.0, (BATCH, SEQ, width), jnp.float32)
    return result.astype(jnp.bfloat16)


def shard_levels(key, extent, cuts, smallest, top_value):
    level, own = 1.0, jax.random.fold_in(key, 6)
    for axis_at, shards_of in cuts:
        heights = jnp.exp(jax.random.uniform(jax.random.fold_in(own, axis_at), (shards_of,), jnp.float32, smallest / len(cuts), top_value / len(cuts)))
        level = level * jnp.repeat(heights, extent[axis_at] // shards_of).reshape([-1 if axis == axis_at else 1 for axis in range(len(extent))])
    return level


def bell_draw(rng, dims, scale, bound, cuts=(), kind=jnp.bfloat16):
    drawn = scale * jax.random.normal(rng, dims, jnp.float32)
    if cuts:
        drawn = drawn * shard_levels(rng, dims, cuts, -0.22, 0.18)
    return jnp.clip(drawn, -bound, bound).astype(kind)


def setup_inputs(seed: int = 0) -> dict:
    streams_of = jax.random.split(jax.random.key(seed), 6)
    return {
        "queries": draw_queries(jax.random.fold_in(streams_of[5], 71), 0),
        "keys": draw_keys(jax.random.fold_in(streams_of[5], 71), 0),
        "values": bell_draw(streams_of[2], (BATCH, SEQ, HE), 1.0, 6.0, ((0, 8), (1, 32))),
        "grad_out": bell_draw(streams_of[3], (BATCH, SEQ, DMODEL), 1.0, 6.0, ((0, 8), (1, 32))),
        "out_weight": bell_draw(streams_of[4], (HE, DMODEL), HEAD ** -0.5, 0.5),
    }


def pooled(rows):
    shape = rows.shape
    grouped = rows.astype(jnp.float32).reshape(shape[:-2] + (shape[-2] // POOL, POOL, shape[-1]))
    return (lax.optimization_barrier(jnp.sum(grouped, axis=-2)) * (1.0 / math.sqrt(POOL))).astype(jnp.bfloat16)

def allowed_keys(device, tokens, devices):
    device = device.astype(jnp.int32)
    seq_len = tokens * devices
    blocks = seq_len // BLOCK
    group_rows = GROUP * tokens // POOL
    group = device // GROUP
    qblock = ((device * tokens + jnp.arange(tokens, dtype=jnp.int32)) // BLOCK)[:, None]
    fine_tok = device * tokens - BLOCK + jnp.arange(tokens + 2 * BLOCK, dtype=jnp.int32)
    fine_block = fine_tok // BLOCK
    fine_ok = (fine_tok >= 0)[None, :] & (fine_tok < seq_len)[None, :] & (jnp.abs(fine_block[None, :] - qblock) <= 1)
    one_index = group * group_rows + jnp.arange(group_rows, dtype=jnp.int32)
    one_block = one_index * POOL // BLOCK
    one_ok = jnp.abs(one_block[None, :] - qblock) > 1
    two_block = jnp.arange(blocks, dtype=jnp.int32)
    two_ok = (two_block // (GROUP * tokens // BLOCK) != group)[None, :] & (jnp.abs(two_block[None, :] - qblock) > 1)
    return jnp.concatenate([fine_ok, one_ok, two_ok], axis=1)

def heads_pass(query_rows, key_rows, value_rows, grad_rows, allowed):
    tokens = query_rows.shape[0]
    width = query_rows.shape[1]
    count = key_rows.shape[0]
    factor = 1.0 / math.sqrt(HEAD)

    def one_head(head, carry):
        attn, grad_q, grad_k, grad_v = carry
        begin = head * HEAD
        qhead = lax.dynamic_slice_in_dim(query_rows, begin, HEAD, 1)
        khead = lax.dynamic_slice_in_dim(key_rows, begin, HEAD, 1)
        vhead = lax.dynamic_slice_in_dim(value_rows, begin, HEAD, 1)
        ghead = lax.dynamic_slice_in_dim(grad_rows, begin, HEAD, 1)
        scores = lax.dot_general(qhead, khead, (((1,), (1,)), ((), ())), preferred_element_type=jnp.float32) * factor
        scores = jnp.where(allowed, scores, -jnp.inf)
        top = lax.optimization_barrier(jnp.max(scores, axis=1, keepdims=True))
        weights = jnp.where(allowed, jnp.exp(scores - top), 0.0)
        probs = weights / lax.optimization_barrier(jnp.sum(weights, axis=1, keepdims=True))
        probs_low = probs.astype(jnp.bfloat16)
        ohead = jnp.dot(probs_low, vhead, preferred_element_type=jnp.float32).astype(jnp.bfloat16)
        dprob = lax.dot_general(ghead, vhead, (((1,), (1,)), ((), ())), preferred_element_type=jnp.float32)
        delta = lax.optimization_barrier(jnp.sum(ghead.astype(jnp.float32) * ohead.astype(jnp.float32), axis=1, keepdims=True))
        dscore = (probs * (dprob - delta)).astype(jnp.bfloat16)
        dqhead = (jnp.dot(dscore, khead, preferred_element_type=jnp.float32) * factor).astype(jnp.bfloat16)
        dkhead = lax.dot_general(dscore, qhead, (((0,), (0,)), ((), ())), preferred_element_type=jnp.float32) * factor
        dvhead = lax.dot_general(probs_low, ghead, (((0,), (0,)), ((), ())), preferred_element_type=jnp.float32)
        attn = lax.dynamic_update_slice_in_dim(attn, ohead, begin, 1)
        grad_q = lax.dynamic_update_slice_in_dim(grad_q, dqhead, begin, 1)
        grad_k = lax.dynamic_update_slice_in_dim(grad_k, dkhead, begin, 1)
        grad_v = lax.dynamic_update_slice_in_dim(grad_v, dvhead, begin, 1)
        return (attn, grad_q, grad_k, grad_v)
    start_state = (jnp.zeros((tokens, width), jnp.bfloat16), jnp.zeros((tokens, width), jnp.bfloat16), jnp.zeros((count, width), jnp.float32), jnp.zeros((count, width), jnp.float32))
    return lax.fori_loop(0, width // HEAD, one_head, start_state)

def assemble(parts, tokens):
    width = parts.shape[2]
    span = tokens + 2 * BLOCK
    group_rows = GROUP * tokens // POOL
    fine = parts[:, :span]
    own = fine[:, BLOCK:BLOCK + tokens]
    own = own.at[:-1, tokens - BLOCK:].add(fine[1:, :BLOCK])
    own = own.at[1:, :BLOCK].add(fine[:-1, tokens + BLOCK:])
    level_one = parts[:, span:span + group_rows]
    level_two = lax.optimization_barrier(jnp.sum(parts[:, span + group_rows:], axis=0))
    groups = N_CTX // GROUP
    rows_one = lax.optimization_barrier(jnp.sum(level_one.reshape(groups, GROUP, group_rows, width), axis=1)).reshape(groups * group_rows, width)
    scale = 1.0 / math.sqrt(POOL)
    rows_one = rows_one + jnp.repeat(level_two * scale, POOL, axis=0)
    total = own.reshape(N_CTX * tokens, width) + jnp.repeat(rows_one * scale, POOL, axis=0)
    return total.astype(jnp.bfloat16)

def reference(queries, keys, values, grad_out, out_weight):
    tokens = TOK_DEV
    seq_len = tokens * N_CTX
    group_rows = GROUP * tokens // POOL

    def one_sequence(inputs):
        query_rows, key_rows, value_rows, upstream = inputs
        width = query_rows.shape[1]
        backward = jnp.dot(upstream, out_weight.T, preferred_element_type=jnp.float32).astype(jnp.bfloat16)
        key_one = pooled(key_rows)
        value_one = pooled(value_rows)
        key_two = pooled(key_one)
        value_two = pooled(value_one)
        padding = jnp.zeros((BLOCK, width), key_rows.dtype)
        key_pad = jnp.concatenate([padding, key_rows, padding], axis=0)
        value_pad = jnp.concatenate([padding, value_rows, padding], axis=0)

        def device_block(device):
            first = device * tokens
            qpart = lax.dynamic_slice_in_dim(query_rows, first, tokens, 0)
            gpart = lax.dynamic_slice_in_dim(backward, first, tokens, 0)
            begin = device // GROUP * group_rows
            key_all = jnp.concatenate([lax.dynamic_slice_in_dim(key_pad, first, tokens + 2 * BLOCK, 0), lax.dynamic_slice_in_dim(key_one, begin, group_rows, 0), key_two], axis=0)
            value_all = jnp.concatenate([lax.dynamic_slice_in_dim(value_pad, first, tokens + 2 * BLOCK, 0), lax.dynamic_slice_in_dim(value_one, begin, group_rows, 0), value_two], axis=0)
            return heads_pass(qpart, key_all, value_all, gpart, allowed_keys(device, tokens, N_CTX))
        attn, grad_q, grad_k, grad_v = lax.map(device_block, jnp.arange(N_CTX, dtype=jnp.int32))
        attn_rows = attn.reshape(seq_len, width)
        mixed = jnp.dot(attn_rows, out_weight, preferred_element_type=jnp.float32).astype(jnp.bfloat16)
        weight_part = jnp.dot(attn_rows.T, upstream, preferred_element_type=jnp.float32)
        return (mixed, grad_q.reshape(seq_len, width), assemble(grad_k, tokens), assemble(grad_v, tokens), weight_part)
    mixed, grad_queries, grad_keys, grad_values, weight_parts = lax.map(one_sequence, (queries, keys, values, grad_out))
    return (mixed, grad_queries, grad_keys, grad_values, lax.optimization_barrier(jnp.sum(weight_parts, axis=0)))
```

```python
import functools
import math

import jax
import jax.numpy as jnp
from jax import lax
from jax.experimental import pallas as pl
from jax.experimental.pallas import tpu as pltpu
from jax.sharding import PartitionSpec as P

HEAD = 128
BLOCK = 256
POOL = 16
GROUP = 8
SCALE = 1.0 / math.sqrt(POOL)
FACTOR = 1.0 / math.sqrt(HEAD)
LOG2E = math.log2(math.e)
MASKED = -1e30
F32 = jnp.float32
BF16 = jnp.bfloat16


def dot(a, b, da, db):
    return lax.dot_general(a, b, (((da,), (db,)), ((), ())), preferred_element_type=F32)


def parts_of(side, mem, which):
    own, before, after, one, two = mem
    near = (before, after)[side]
    ones = one[:, which].reshape(-1, HEAD)
    twos = two[:, which].reshape(-1, HEAD)
    return own[...], near[which], ones, twos


def scores_of(side, q, keys, edge_ref, bias_ref):
    own, near, ones, twos = keys
    n1 = ones.shape[0]
    s_own = dot(own, q, 1, 1) * (FACTOR * LOG2E)
    s_near = dot(near, q, 1, 1) * (FACTOR * LOG2E) + edge_ref[side]
    s_one = dot(ones, q, 1, 1) * (FACTOR * LOG2E) + bias_ref[side, :n1]
    s_two = dot(twos, q, 1, 1) * (FACTOR * LOG2E) + bias_ref[side, n1:]
    return s_own, s_near, s_one, s_two


def forward_kernel(edge_ref, bias_ref, q_ref, k_ref, v_ref, g_ref, before, after, one, two, attn_ref, stat_ref):
    for side in range(2):
        rows = pl.ds(side * BLOCK, BLOCK)
        q = q_ref[rows, :]
        keys = parts_of(side, (k_ref, before, after, one, two), 0)
        values = parts_of(side, (v_ref, before, after, one, two), 1)
        scores = scores_of(side, q, keys, edge_ref, bias_ref)
        top = functools.reduce(jnp.maximum, [jnp.max(s, axis=0, keepdims=True) for s in scores])
        total = 0.0
        out = 0.0
        for s, v in zip(scores, values):
            p = jnp.exp2(s - top)
            total = total + jnp.sum(p, axis=0, keepdims=True)
            out = out + dot(v, p.astype(BF16), 0, 0)
        out = jnp.transpose(out / total).astype(BF16)
        attn_ref[rows, :] = out
        stat_ref[0, 0:1, rows] = top + jnp.log2(total)
        g = g_ref[rows, :].astype(F32)
        stat_ref[0, 1:2, rows] = jnp.sum(jnp.transpose(g * out.astype(F32)), axis=0, keepdims=True)


def backward_kernel(
    edge_ref, bias_ref, q_ref, k_ref, v_ref, g_ref, before, after, one, two, stat_ref,
    dq_ref, down_ref, dbefore_ref, dafter_ref, done_ref, dtwo_ref,
):
    n1 = one.shape[0] * one.shape[2]
    for side in range(2):
        rows = pl.ds(side * BLOCK, BLOCK)
        q = q_ref[rows, :]
        g = g_ref[rows, :]
        keys = parts_of(side, (k_ref, before, after, one, two), 0)
        values = parts_of(side, (v_ref, before, after, one, two), 1)
        scores = scores_of(side, q, keys, edge_ref, bias_ref)
        lse = stat_ref[0, 0:1, rows]
        delta = stat_ref[0, 1:2, rows]
        dq = 0.0
        grads = []
        for s, k, v in zip(scores, keys, values):
            p = jnp.exp2(s - lse)
            dp = dot(v, g, 1, 1)
            ds = (p * (dp - delta)).astype(BF16)
            dq = dq + dot(k, ds, 0, 0)
            grads.append((dot(ds, q, 1, 0) * FACTOR, dot(p.astype(BF16), g, 1, 0)))
        dq_ref[rows, :] = jnp.transpose(dq * FACTOR).astype(BF16)
        near_ref = (dbefore_ref, dafter_ref)[side]
        for which in range(2):
            d_own, d_near, d_one, d_two = (pair[which] for pair in grads)
            near_ref[which] = d_near.astype(BF16)
            if side == 0:
                down_ref[which] = d_own
                done_ref[which] = d_one
                dtwo_ref[which] = d_two
            else:
                down_ref[which] += d_own
                done_ref[which] += d_one
                dtwo_ref[which] += d_two


def head_specs(tokens, one, two):
    col = lambda *lead: pl.BlockSpec(lead + (HEAD,), lambda h: (0,) * len(lead) + (h,))
    rows = col(tokens)
    near = col(2, BLOCK)
    return rows, near, col(one.shape[0], 2, one.shape[2]), col(two.shape[0], 2, two.shape[2]), col


PARAMS = pltpu.CompilerParams(vmem_limit_bytes=40 * 1024 * 1024)


def forward_heads(edge, bias, q, k, v, g, before, after, one, two):
    tokens, width = q.shape
    heads = width // HEAD
    rows, near, ones, twos, col = head_specs(tokens, one, two)
    stat = pl.BlockSpec((1, 2, tokens), lambda h: (h, 0, 0))
    return pl.pallas_call(
        forward_kernel,
        grid=(heads,),
        in_specs=[
            pl.BlockSpec(memory_space=pltpu.SMEM),
            pl.BlockSpec(bias.shape, lambda h: (0, 0, 0)),
            rows, rows, rows, rows, near, near, ones, twos,
        ],
        out_specs=[rows, stat],
        out_shape=[
            jax.ShapeDtypeStruct((tokens, width), BF16),
            jax.ShapeDtypeStruct((heads, 2, tokens), F32),
        ],
        compiler_params=PARAMS,
        name="forward_heads",
    )(edge, bias, q, k, v, g, before, after, one, two)


def backward_heads(edge, bias, q, k, v, g, before, after, one, two, stats):
    tokens, width = q.shape
    heads = width // HEAD
    rows, near, ones, twos, col = head_specs(tokens, one, two)
    stat = pl.BlockSpec((1, 2, tokens), lambda h: (h, 0, 0))
    n1, n2 = one.shape[0] * one.shape[2], two.shape[0] * two.shape[2]
    return pl.pallas_call(
        backward_kernel,
        grid=(heads,),
        in_specs=[
            pl.BlockSpec(memory_space=pltpu.SMEM),
            pl.BlockSpec(bias.shape, lambda h: (0, 0, 0)),
            rows, rows, rows, rows, near, near, ones, twos, stat,
        ],
        out_specs=[rows, col(2, tokens), near, near, col(2, n1), col(2, n2)],
        out_shape=[
            jax.ShapeDtypeStruct((tokens, width), BF16),
            jax.ShapeDtypeStruct((2, tokens, width), F32),
            jax.ShapeDtypeStruct((2, BLOCK, width), BF16),
            jax.ShapeDtypeStruct((2, BLOCK, width), BF16),
            jax.ShapeDtypeStruct((2, n1, width), F32),
            jax.ShapeDtypeStruct((2, n2, width), F32),
        ],
        compiler_params=PARAMS,
        name="backward_heads",
    )(edge, bias, q, k, v, g, before, after, one, two, stats)


def exchange(x, axis, groups=None):
    return lax.all_to_all(x, axis, 0, 0, axis_index_groups=groups, tiled=True)


def pooled(rows):
    shape = rows.shape
    grouped = rows.astype(F32).reshape(shape[:-2] + (shape[-2] // POOL, POOL, shape[-1]))
    return (jnp.sum(grouped, axis=-2) * SCALE).astype(BF16)


def masks(device, devices, tokens):
    group = device // GROUP
    per_group = GROUP * tokens // BLOCK
    block = device * (tokens // BLOCK) + jnp.arange(2, dtype=jnp.int32)[:, None]
    one = group * per_group + jnp.arange(GROUP * tokens // POOL, dtype=jnp.int32) * POOL // BLOCK
    two = jnp.arange(devices * tokens // BLOCK, dtype=jnp.int32)
    one_ok = jnp.abs(one[None] - block) > 1
    two_ok = (jnp.abs(two[None] - block) > 1) & (two // per_group != group)[None]
    ok = jnp.concatenate([one_ok, two_ok], axis=1)
    bias = jnp.where(ok, 0.0, MASKED).astype(F32)
    bias = jnp.broadcast_to(bias[:, :, None], bias.shape + (BLOCK,))
    edge = jnp.stack([device == 0, device == devices - 1]).astype(F32) * MASKED
    return edge, bias


def on_device(queries, keys, values, grad_out, out_weight):
    q, k, v, upstream = queries[0], keys[0], values[0], grad_out[0]
    tokens, width = q.shape
    devices = lax.axis_size("ctx")
    dp = lax.axis_size("dp")
    device = lax.axis_index("ctx")
    groups = devices // GROUP
    near = [[g * GROUP + i for i in range(GROUP)] for g in range(groups)]
    far = [[g * GROUP + i for g in range(groups)] for i in range(GROUP)]
    up = [(i, i + 1) for i in range(devices - 1)]
    down = [(i + 1, i) for i in range(devices - 1)]
    rows_one = tokens // POOL
    rows_two = tokens // BLOCK

    before = lax.ppermute(jnp.stack([k[tokens - BLOCK :], v[tokens - BLOCK :]]), "ctx", up)
    after = lax.ppermute(jnp.stack([k[:BLOCK], v[:BLOCK]]), "ctx", down)
    local_one = jnp.stack([pooled(k), pooled(v)])
    one = exchange(jnp.broadcast_to(local_one[None], (GROUP,) + local_one.shape), "ctx", near)
    group_two = jnp.swapaxes(pooled(one), 0, 1).reshape(2, GROUP * rows_two, width)
    two = exchange(jnp.broadcast_to(group_two[None], (groups,) + group_two.shape), "ctx", far)

    edge, bias = masks(device, devices, tokens)
    g = dot(upstream, out_weight, 1, 1).astype(BF16)
    attn, stats = forward_heads(edge, bias, q, k, v, g, before, after, one, two)

    partial = dot(attn, upstream, 0, 0).astype(BF16)
    share = width // (devices * dp)
    partial = partial.reshape(groups, GROUP, dp, share, width).transpose(2, 0, 1, 3, 4)
    summed = lax.psum_scatter(partial, "dp", scatter_dimension=0, tiled=False)
    mixed = jnp.dot(attn, out_weight, preferred_element_type=F32).astype(BF16)

    dq, d_own, d_before, d_after, d_one, d_two = backward_heads(
        edge, bias, q, k, v, g, before, after, one, two, stats
    )
    from_after = lax.ppermute(d_before, "ctx", down)
    from_before = lax.ppermute(d_after, "ctx", up)

    d_two = d_two.astype(BF16).reshape(2, groups, GROUP * rows_two, width).transpose(1, 0, 2, 3)
    weight_far = summed.astype(BF16).reshape(groups, GROUP * share, width)
    packed = jnp.concatenate([d_two.reshape(groups, -1, width), weight_far], axis=1)
    packed = jnp.sum(exchange(packed, "ctx", far).astype(F32), axis=0)
    n2 = 2 * GROUP * rows_two
    mine_two = packed[:n2].reshape(2, GROUP * rows_two, 1, width)
    d_one = d_one.reshape(2, GROUP * rows_two, POOL, width) + mine_two * SCALE
    d_one = d_one.astype(BF16).reshape(2, GROUP, rows_one, width).transpose(1, 0, 2, 3)
    weight_near = packed[n2:].astype(BF16).reshape(GROUP, share, width)
    packed = jnp.concatenate([d_one.reshape(GROUP, -1, width), weight_near], axis=1)
    packed = jnp.sum(exchange(packed, "ctx", near).astype(F32), axis=0)
    mine_one = packed[: 2 * rows_one].reshape(2, rows_one, 1, width)
    mine_weight = packed[2 * rows_one :].astype(BF16)
    grad_weight = exchange(jnp.broadcast_to(mine_weight[None], (dp, share, width)), "dp")
    grad_weight = grad_weight.reshape(dp * share, width).astype(F32)

    total = d_own.reshape(2, rows_one, POOL, width) + mine_one * SCALE
    total = total.reshape(2, tokens, width)
    head = total[:, :BLOCK] + from_before.astype(F32)
    tail = total[:, tokens - BLOCK :] + from_after.astype(F32)
    total = jnp.concatenate([head, tail], axis=1).astype(BF16)
    return mixed[None], dq[None], total[0][None], total[1][None], grad_weight


def solution(mesh):
    rows = P("dp", "ctx", None)
    return jax.shard_map(
        on_device,
        mesh=mesh,
        in_specs=(rows, rows, rows, rows, P()),
        out_specs=(rows, rows, rows, rows, P("ctx", None)),
        check_vma=False,
    )
```

```python
import math

import jax
import jax.numpy as jnp
from jax import lax
from jax.experimental import pallas as pl
from jax.experimental.pallas import tpu as pltpu
from jax.sharding import PartitionSpec as P

HEAD = 128
BLOCK = 256
POOL = 16
GROUP = 8
SCALE = 1.0 / math.sqrt(POOL)
FACTOR = 1.0 / math.sqrt(HEAD)
LOG2 = FACTOR * math.log2(math.e)
MASKED = -1e30
F32 = jnp.float32
BF16 = jnp.bfloat16
PER = (2, 2, 2, 2, 2, 2, 4, 2)
PARAMS = pltpu.CompilerParams(vmem_limit_bytes=56 * 1024 * 1024)


def dot(a, b, da, db):
    return lax.dot_general(a, b, (((da,), (db,)), ((), ())), preferred_element_type=F32)


def shape(dims, kind):
    return jax.ShapeDtypeStruct(dims, kind)


def cols(*lead, width=HEAD):
    def spec(per):
        return pl.BlockSpec(lead + (width * per,), lambda h: (0,) * len(lead) + (h,))

    return spec, lambda ref, i: ref.at[(slice(None),) * len(lead) + (pl.ds(i * width, width),)]


def heads_of(*dims):
    def spec(per):
        return pl.BlockSpec((per,) + dims, lambda h: (h,) + (0,) * len(dims))

    return spec, lambda ref, i: ref.at[pl.ds(i, 1)]


def second(lead, rows, *rest):
    def spec(per):
        return pl.BlockSpec((lead, rows * per) + rest, lambda h: (0, h) + (0,) * len(rest))

    return spec, lambda ref, i: ref.at[:, pl.ds(i * rows, rows)]


def leading(rows, *rest):
    def spec(per):
        return pl.BlockSpec((rows * per,) + rest, lambda h: (h,) + (0,) * len(rest))

    return spec, lambda ref, i: ref.at[pl.ds(i * rows, rows)]


def fixed(*dims):
    return lambda per: pl.BlockSpec(dims, lambda h: (0,) * len(dims)), lambda ref, i: ref


SMEM = lambda per: pl.BlockSpec(memory_space=pltpu.SMEM), lambda ref, i: ref


def over_heads(kernel, steps, per, ins, outs, out_shape, name, flops=1):
    def body(*refs):
        for i in range(per):
            kernel(*(view(ref, i) for ref, (_, view) in zip(refs, ins + outs)))

    return pl.pallas_call(
        body,
        grid=(steps // per,),
        in_specs=[spec(per) for spec, _ in ins],
        out_specs=[spec(per) for spec, _ in outs],
        out_shape=out_shape,
        compiler_params=PARAMS,
        cost_estimate=pl.CostEstimate(flops=flops, bytes_accessed=1, transcendentals=0),
        name=name,
    )


def prepare_kernel(k_ref, v_ref, last_ref, first_ref, one_ref):
    tokens = k_ref.shape[0]
    count = tokens // POOL
    row = lax.broadcasted_iota(jnp.int32, (count, tokens), 0)
    at = lax.broadcasted_iota(jnp.int32, (count, tokens), 1)
    member = (at // POOL == row).astype(BF16)
    for which, ref in enumerate((k_ref, v_ref)):
        rows = ref[...]
        last_ref[which] = rows[tokens - BLOCK :]
        first_ref[which] = rows[:BLOCK]
        one = (dot(member, rows, 1, 0) * SCALE).astype(BF16)
        for slot in range(GROUP):
            one_ref[slot, which * count : (which + 1) * count] = one


def prepare(k, v):
    tokens, width = k.shape
    step = 2 * HEAD
    rows = cols(tokens, width=step)
    edge = cols(2, BLOCK, width=step)
    return over_heads(
        prepare_kernel,
        width // step,
        PER[0],
        [rows, rows],
        [edge, edge, cols(GROUP, 2 * tokens // POOL, width=step)],
        [
            shape((2, BLOCK, width), BF16),
            shape((2, BLOCK, width), BF16),
            shape((GROUP, 2 * tokens // POOL, width), BF16),
        ],
        "prepare",
    )(k, v)


def both(left, right):
    return jnp.concatenate([left, right], axis=1)


def near_scores(edge_ref, before, after, q):
    first = dot(before[0], q[:BLOCK], 1, 1) * LOG2 + edge_ref[0]
    return both(first, dot(after[0], q[BLOCK:], 1, 1) * LOG2 + edge_ref[1])


def join(stat_ref, acc_ref, s):
    own_top = stat_ref[0, 0:1]
    top = jnp.maximum(own_top, jnp.max(s, axis=0, keepdims=True))
    shrink = jnp.exp2(own_top - top)
    p = jnp.exp2(s - top)
    total = stat_ref[0, 1:2] * shrink + jnp.sum(p, axis=0, keepdims=True)
    return top, total, acc_ref[0] * shrink, p.astype(BF16)


def own_kernel(q_ref, k_ref, v_ref, acc_ref, stat_ref):
    s = dot(k_ref[...], q_ref[...], 1, 1) * LOG2
    top = jnp.max(s, axis=0, keepdims=True)
    p = jnp.exp2(s - top)
    stat_ref[0, 0:1] = top
    stat_ref[0, 1:2] = jnp.sum(p, axis=0, keepdims=True)
    acc_ref[0] = dot(v_ref[...], p.astype(BF16), 0, 0)


def forward_own(q, k, v):
    tokens, width = q.shape
    heads = width // HEAD
    rows = cols(tokens)
    return over_heads(
        own_kernel,
        heads,
        PER[1],
        [rows, rows, rows],
        [heads_of(HEAD, tokens), heads_of(2, tokens)],
        [shape((heads, HEAD, tokens), F32), shape((heads, 2, tokens), F32)],
        "forward_own",
    )(q, k, v)


def coarse_rows(one, two):
    half = one.shape[1] // 2
    middle = [one[:, which * half : (which + 1) * half].reshape(-1, HEAD) for which in range(2)]
    groups, per_group, _ = two.shape
    count = groups * per_group
    pairs = per_group // (2 * GROUP)
    to = lax.broadcasted_iota(jnp.int32, (count, count), 0)
    at = lax.broadcasted_iota(jnp.int32, (count, count), 1)
    member = to // (pairs * groups) % GROUP
    source = to // pairs % groups * per_group + member * 2 * pairs + to // (count // 2) * pairs + to % pairs
    top = dot((at == source).astype(BF16), two[...].reshape(count, HEAD), 1, 0).astype(BF16)
    keys = jnp.concatenate([middle[0], top[: count // 2]], axis=0)
    values = jnp.concatenate([middle[1], top[count // 2 :]], axis=0)
    return keys, values


def forward_coarse_kernel(bias_ref, q_ref, one, two, acc_ref, stat_ref, out_ref, new_ref):
    keys, values = coarse_rows(one, two)
    s = dot(keys, q_ref[...], 1, 1) * LOG2 + bias_ref[...]
    top, total, out, p = join(stat_ref, acc_ref, s)
    new_ref[0, 0:1] = top
    new_ref[0, 1:2] = total
    out_ref[0] = out + dot(values, p, 0, 0)


def forward_coarse(bias, q, one, two, acc, stat):
    tokens, width = q.shape
    heads = width // HEAD
    state = [heads_of(HEAD, tokens), heads_of(2, tokens)]
    return over_heads(
        forward_coarse_kernel,
        heads,
        PER[3],
        [fixed(*bias.shape), cols(tokens), cols(*one.shape[:2]), cols(*two.shape[:2])] + state,
        state,
        [shape((heads, HEAD, tokens), F32), shape((heads, 2, tokens), F32)],
        "forward_coarse",
    )(bias, q, one, two, acc, stat)


def forward_near_kernel(
    edge_ref, q_ref, g_ref, before, after, acc_ref, own_ref, attn_ref, across_ref, stat_ref
):
    s = near_scores(edge_ref, before, after, q_ref[...])
    top, total, out, p = join(own_ref, acc_ref, s)
    out = out + both(dot(before[1], p[:, :BLOCK], 0, 0), dot(after[1], p[:, BLOCK:], 0, 0))
    across = (out / total).astype(BF16)
    across_ref[...] = across
    attn_ref[...] = jnp.transpose(across.astype(F32)).astype(BF16)
    stat_ref[0, 0:1] = top + jnp.log2(total)
    stat_ref[0, 1:2] = jnp.sum(jnp.transpose(g_ref[...].astype(F32)) * across.astype(F32), axis=0, keepdims=True)


def forward_near(edge, q, g, before, after, acc, stat):
    tokens, width = q.shape
    heads = width // HEAD
    rows = cols(tokens)
    near = cols(2, BLOCK)
    return over_heads(
        forward_near_kernel,
        heads,
        PER[2],
        [SMEM, rows, rows, near, near, heads_of(HEAD, tokens), heads_of(2, tokens)],
        [rows, leading(HEAD, tokens), heads_of(2, tokens)],
        [
            shape((tokens, width), BF16),
            shape((width, tokens), BF16),
            shape((heads, 2, tokens), F32),
        ],
        "forward_near",
    )(edge, q, g, before, after, acc, stat)


def weight_kernel(core_ref, across_ref, up_ref, keep_ref, send_ref):
    weight = dot(across_ref[...], up_ref[...], 1, 0).astype(BF16)
    first = core_ref[0] == 0
    keep_ref[0] = jnp.where(first, weight[:, :HEAD], weight[:, HEAD:])
    send_ref[0] = jnp.where(first, weight[:, HEAD:], weight[:, :HEAD])


def weight_terms(core, across, upstream):
    width, tokens = across.shape
    model = upstream.shape[1]
    pairs = model // (2 * HEAD)
    return over_heads(
        weight_kernel,
        pairs,
        PER[7],
        [SMEM, fixed(width, tokens), cols(tokens, width=2 * HEAD)],
        [leading(1, width, HEAD)] * 2,
        [shape((pairs, width, HEAD), BF16)] * 2,
        "weight_terms",
    )(core, across, upstream)


def gradients(s, dprob, stat_ref):
    p = jnp.exp2(s - stat_ref[0, 0:1])
    return p.astype(BF16), (p * (dprob - stat_ref[0, 1:2])).astype(BF16)


def backward_coarse_kernel(bias_ref, q_ref, g_ref, one, two, stat_ref, part_ref, dq_ref, one_ref, two_ref):
    keys, values = coarse_rows(one, two)
    q, g = q_ref[...], g_ref[...]
    s = dot(keys, q, 1, 1) * LOG2 + bias_ref[...]
    p, ds = gradients(s, dot(values, g, 1, 1), stat_ref)
    dk = dot(ds, q, 1, 0) * FACTOR
    dv = dot(p, g, 1, 0)
    dq_ref[...] = jnp.transpose((part_ref[0] + dot(keys, ds, 0, 0)) * FACTOR).astype(BF16)
    slots = one_ref.shape[0]
    count = slots * (one_ref.shape[2] // 2)
    for ref, begin, end in ((one_ref, 0, count), (two_ref, count, dk.shape[0])):
        pieces = [d[begin:end].reshape(slots, -1, HEAD) for d in (dk, dv)]
        ref[:, 0] = jnp.concatenate(pieces, axis=1).astype(BF16)


def backward_coarse(bias, q, g, one, two, stat, part):
    tokens, width = q.shape
    heads = width // HEAD
    rows = cols(tokens)
    slots = one.shape[0]
    for_one, for_two = one.shape[1], two.shape[0] * two.shape[1] // slots
    return over_heads(
        backward_coarse_kernel,
        heads,
        PER[5],
        [
            fixed(*bias.shape), rows, rows, cols(*one.shape[:2]), cols(*two.shape[:2]), heads_of(2, tokens),
            heads_of(HEAD, tokens),
        ],
        [rows, second(slots, 1, for_one, HEAD), second(slots, 1, for_two, HEAD)],
        [
            shape((tokens, width), BF16),
            shape((slots, heads, for_one, HEAD), BF16),
            shape((slots, heads, for_two, HEAD), BF16),
        ],
        "backward_coarse",
    )(bias, q, g, one, two, stat, part)


def fine_kernel(
    edge_ref, q_ref, k_ref, v_ref, g_ref, before, after, stat_ref, part_ref, down_ref, dbefore_ref, dafter_ref
):
    q, k, v, g = q_ref[...], k_ref[...], v_ref[...], g_ref[...]
    s_near = near_scores(edge_ref, before, after, q)
    dp_near = both(dot(before[1], g[:BLOCK], 1, 1), dot(after[1], g[BLOCK:], 1, 1))
    p_near, ds_near = gradients(s_near, dp_near, stat_ref)
    p, ds = gradients(dot(k, q, 1, 1) * LOG2, dot(v, g, 1, 1), stat_ref)
    down_ref[0] = dot(ds, q, 1, 0) * FACTOR
    down_ref[1] = dot(p, g, 1, 0)
    near = both(dot(before[0], ds_near[:, :BLOCK], 0, 0), dot(after[0], ds_near[:, BLOCK:], 0, 0))
    part_ref[0] = near + dot(k, ds, 0, 0)
    for side, ref in enumerate((dbefore_ref, dafter_ref)):
        rows = slice(side * BLOCK, (side + 1) * BLOCK)
        ref[0] = (dot(ds_near[:, rows], q[rows], 1, 0) * FACTOR).astype(BF16)
        ref[1] = dot(p_near[:, rows], g[rows], 1, 0).astype(BF16)


def backward_fine(edge, q, k, v, g, before, after, stat):
    tokens, width = q.shape
    heads = width // HEAD
    rows = cols(tokens)
    near = cols(2, BLOCK)
    return over_heads(
        fine_kernel,
        heads,
        PER[4],
        [SMEM, rows, rows, rows, rows, near, near, heads_of(2, tokens)],
        [heads_of(HEAD, tokens), cols(2, tokens), near, near],
        [
            shape((heads, HEAD, tokens), F32),
            shape((2, tokens, width), F32),
            shape((2, BLOCK, width), BF16),
            shape((2, BLOCK, width), BF16),
        ],
        "backward_fine",
    )(edge, q, k, v, g, before, after, stat)


def project_kernel(attn_ref, weight_ref, out_ref):
    out_ref[...] = dot(attn_ref[...], weight_ref[...], 1, 0).astype(BF16)


def project(attn, weight):
    tokens, width = attn.shape
    model = weight.shape[1]
    step = 2 * HEAD
    return over_heads(
        project_kernel,
        model // step,
        1,
        [fixed(tokens, width), cols(width, width=step)],
        [cols(tokens, width=step)],
        [shape((tokens, model), BF16)],
        "project",
    )(attn, weight)[0]


def finish_kernel(own, first, last, one_ref, two_ref, dk_ref, dv_ref):
    tokens = own.shape[1]
    size = tokens // POOL
    one = jnp.sum(one_ref[...].astype(F32), axis=0)
    for which, out_ref in enumerate((dk_ref, dv_ref)):
        term = one[which * size : (which + 1) * size] * SCALE
        term = jnp.broadcast_to(term[:, None], (size, POOL, HEAD)).reshape(tokens, HEAD)
        for side, edge in enumerate((first, last)):
            rows = pl.ds(side * BLOCK, BLOCK)
            at = 2 * which + side
            top = two_ref[0, at : at + 1] * (SCALE * SCALE)
            total = own[which, rows] + term[side * BLOCK : (side + 1) * BLOCK] + top + edge[which].astype(F32)
            out_ref[rows, :] = total.astype(BF16)


def finish(own, first, last, one, two):
    tokens, width = own.shape[1:]
    rows = 2 * tokens // POOL
    return over_heads(
        finish_kernel,
        width // HEAD,
        PER[6],
        [
            cols(2, tokens), cols(2, BLOCK), cols(2, BLOCK),
            second(one.shape[0], rows, HEAD), heads_of(*two.shape[1:]),
        ],
        [cols(tokens)] * 2,
        [shape((tokens, width), BF16)] * 2,
        "finish",
    )(own, first, last, one, two)


def exchange(x, axis, groups=None):
    return lax.all_to_all(x, axis, 0, 0, axis_index_groups=groups, tiled=True)


def masks(device, devices, tokens):
    group = device // GROUP
    per_group = GROUP * tokens // BLOCK
    block = device * (tokens // BLOCK) + jnp.arange(2, dtype=jnp.int32)[:, None]
    one = group * per_group + jnp.arange(GROUP * tokens // POOL, dtype=jnp.int32) * POOL // BLOCK
    pairs = tokens // BLOCK
    groups = devices // GROUP
    at = jnp.arange(devices * pairs, dtype=jnp.int32)
    from_group = (group - at // pairs) % groups
    two = from_group * per_group + at // (pairs * groups) * pairs + at % pairs
    one_ok = jnp.abs(one[None] - block) > 1
    two_ok = (jnp.abs(two[None] - block) > 1) & (two // per_group != group)[None]
    ok = jnp.concatenate([one_ok, two_ok], axis=1)
    bias = jnp.where(ok, 0.0, MASKED).astype(F32)
    bias = jnp.repeat(bias.T, BLOCK, axis=1)
    edge = jnp.stack([device == 0, device == devices - 1]).astype(F32) * MASKED
    return edge, bias


def after_all(x, *others):
    return lax.optimization_barrier((x,) + others)[0]


def on_device(queries, keys, values, grad_out, out_weight):
    q, k, v, upstream = queries[0], keys[0], values[0], grad_out[0]
    tokens, width = q.shape
    model = upstream.shape[1]
    devices = lax.axis_size("ctx")
    dp = lax.axis_size("dp")
    device = lax.axis_index("ctx")
    groups = devices // GROUP
    near = [[g * GROUP + i for i in range(GROUP)] for g in range(groups)]
    up = [(i, i + 1) for i in range(devices - 1)]
    down = [(i + 1, i) for i in range(devices - 1)]
    rows_one = tokens // POOL

    pairs = tokens // BLOCK

    far = [[(i, (i + step * GROUP) % devices) for i in range(devices)] for step in range(groups)]
    back = [[(j, i) for i, j in moves] for moves in far]

    last, first, one = prepare(k, v)
    one = exchange(one, "ctx", near)
    edge, bias = masks(device, devices, tokens)
    acc, stat = forward_own(q, k, v)
    one = after_all(one, acc)
    two = one.astype(F32).reshape(GROUP * 2 * pairs, POOL, width)
    two = (jnp.sum(two, axis=1) * SCALE).astype(BF16)
    two = [two] + [lax.ppermute(two, "ctx", moves) for moves in far[1:]]
    g = dot(after_all(upstream, two[0]), out_weight, 1, 1).astype(BF16)
    last, first, two = lax.optimization_barrier((last, first, two, g))[:3]
    before = lax.ppermute(last, "ctx", up)
    after = lax.ppermute(first, "ctx", down)
    two = jnp.stack(two)
    acc, stat = forward_coarse(bias, after_all(q, last), one, two, acc, stat)
    before, after = lax.optimization_barrier((before, after, acc))[:2]
    attn, across, stat = forward_near(edge, q, g, before, after, acc, stat)

    place = lax.axis_index("dp")
    keep, send = weight_terms((place % 2).reshape(1).astype(jnp.int32), across, upstream)
    other = lax.ppermute(send, "dp", [(i, i ^ 1) for i in range(dp)])
    part, d_own, d_before, d_after = backward_fine(
        edge, q, k, v, g, before, after, after_all(stat, send)
    )
    other = after_all(other, d_own)
    shares = []
    for step in range(dp // 2):
        at = (place // 2 + step) % (dp // 2)
        share = lax.dynamic_index_in_dim(keep, at, 0, False).astype(F32)
        share = share + lax.dynamic_index_in_dim(other, at, 0, False).astype(F32)
        shares.append(share.astype(BF16))
    sent = [
        lax.ppermute(share, "dp", [(i, (i + 2 * step) % dp) for i in range(dp)])
        for step, share in enumerate(shares)
        if step
    ]
    from_after = lax.ppermute(d_before, "ctx", down)
    from_before = lax.ppermute(d_after, "ctx", up)
    dq, d_one, d_two = backward_coarse(
        bias, q, lax.optimization_barrier((g, *shares))[0], one, two, stat, part
    )
    sent = lax.optimization_barrier((dq, *sent))[1:]
    weight = sum((share.astype(F32) for share in sent), shares[0].astype(F32)).astype(BF16)
    weight = weight.reshape(groups, GROUP, -1, HEAD).transpose(1, 0, 2, 3).reshape(GROUP, -1, HEAD)

    heads = width // HEAD
    d_one, d_two = d_one.reshape(GROUP, -1, HEAD), d_two.reshape(GROUP, -1, HEAD)
    start, count = d_one.shape[1], d_two.shape[1]
    mixed = project(after_all(attn, dq), out_weight)
    packed = jnp.concatenate([d_one, d_two, weight], axis=1)
    packed = exchange(after_all(packed, from_after, from_before, mixed), "ctx", near)
    small = jnp.sum(packed[:, start:].astype(F32), axis=0).astype(BF16)
    weight = small[count:].reshape(groups, -1, HEAD)
    d_two = small[:count]
    d_two = d_two.reshape(heads, 2, groups, pairs, HEAD).transpose(2, 0, 1, 3, 4).reshape(groups, -1, HEAD)
    count = d_two.shape[1]
    small = []
    for step, moves in enumerate(back):
        at = (device // GROUP - step) % groups
        piece = jnp.concatenate([d_two[step], lax.dynamic_index_in_dim(weight, at, 0, False)], axis=0)
        small.append(lax.ppermute(piece, "ctx", moves) if step else piece)
    small = sum(piece.astype(F32) for piece in small)
    mine_two = small[:count].reshape(heads, 2 * pairs, HEAD)
    weight = small[count:].astype(BF16)
    weight = exchange(jnp.broadcast_to(weight[None], (dp,) + weight.shape), "dp")
    grad_weight = jnp.swapaxes(weight, 0, 1).reshape(-1, model).astype(F32)

    grad_keys, grad_values = finish(d_own, from_before, from_after, packed, mine_two)
    return mixed[None], dq[None], grad_keys[None], grad_values[None], grad_weight


def solution(mesh):
    rows = P("dp", "ctx", None)
    return jax.shard_map(
        on_device,
        mesh=mesh,
        in_specs=(rows, rows, rows, rows, P()),
        out_specs=(rows, rows, rows, rows, P("ctx", None)),
        check_vma=False,
    )
```

```python
import math

import jax
import jax.numpy as jnp
from jax import lax
from jax.experimental import pallas as pl
from jax.experimental.pallas import tpu as pltpu
from jax.sharding import PartitionSpec as P

HEAD = 128
BLOCK = 256
POOL = 16
GROUP = 8
SCALE = 1.0 / math.sqrt(POOL)
FACTOR = 1.0 / math.sqrt(HEAD)
LOG2 = FACTOR * math.log2(math.e)
MASKED = -1e30
F32 = jnp.float32
BF16 = jnp.bfloat16
PER = (2, 2, 2, 2, 2, 2, 4, 2)
PARAMS = pltpu.CompilerParams(vmem_limit_bytes=56 * 1024 * 1024)


def dot(a, b, da, db):
    return lax.dot_general(a, b, (((da,), (db,)), ((), ())), preferred_element_type=F32)


def shape(dims, kind):
    return jax.ShapeDtypeStruct(dims, kind)


def cols(*lead, width=HEAD):
    def spec(per):
        return pl.BlockSpec(lead + (width * per,), lambda h: (0,) * len(lead) + (h,))

    return spec, lambda ref, i: ref.at[(slice(None),) * len(lead) + (pl.ds(i * width, width),)]


def heads_of(*dims):
    def spec(per):
        return pl.BlockSpec((per,) + dims, lambda h: (h,) + (0,) * len(dims))

    return spec, lambda ref, i: ref.at[pl.ds(i, 1)]


def second(lead, rows, *rest):
    def spec(per):
        return pl.BlockSpec((lead, rows * per) + rest, lambda h: (0, h) + (0,) * len(rest))

    return spec, lambda ref, i: ref.at[:, pl.ds(i * rows, rows)]


def leading(rows, *rest):
    def spec(per):
        return pl.BlockSpec((rows * per,) + rest, lambda h: (h,) + (0,) * len(rest))

    return spec, lambda ref, i: ref.at[pl.ds(i * rows, rows)]


def fixed(*dims):
    return lambda per: pl.BlockSpec(dims, lambda h: (0,) * len(dims)), lambda ref, i: ref


SMEM = lambda per: pl.BlockSpec(memory_space=pltpu.SMEM), lambda ref, i: ref


def over_heads(kernel, steps, per, ins, outs, out_shape, name, flops=1):
    def body(*refs):
        for i in range(per):
            kernel(*(view(ref, i) for ref, (_, view) in zip(refs, ins + outs)))

    return pl.pallas_call(
        body,
        grid=(steps // per,),
        in_specs=[spec(per) for spec, _ in ins],
        out_specs=[spec(per) for spec, _ in outs],
        out_shape=out_shape,
        compiler_params=PARAMS,
        cost_estimate=pl.CostEstimate(flops=flops, bytes_accessed=1, transcendentals=0),
        name=name,
    )


def pooling(count, rows):
    row = lax.broadcasted_iota(jnp.int32, (count, rows), 0)
    at = lax.broadcasted_iota(jnp.int32, (count, rows), 1)
    return (at // POOL == row).astype(BF16)


def prepare_kernel(k_ref, v_ref, last_ref, first_ref, one_ref, two_ref):
    tokens = k_ref.shape[0]
    count = tokens // POOL
    tops = []
    for which, ref in enumerate((k_ref, v_ref)):
        rows = ref[...]
        last_ref[which] = rows[tokens - BLOCK :]
        first_ref[which] = rows[:BLOCK]
        one = (dot(pooling(count, tokens), rows, 1, 0) * SCALE).astype(BF16)
        for slot in range(GROUP):
            one_ref[slot, which * count : (which + 1) * count] = one
        tops.append(dot(pooling(8, count), one, 1, 0) * SCALE)
    two_ref[...] = jnp.concatenate(tops, axis=0).astype(BF16)


def prepare(k, v):
    tokens, width = k.shape
    step = 2 * HEAD
    rows = cols(tokens, width=step)
    edge = cols(2, BLOCK, width=step)
    return over_heads(
        prepare_kernel,
        width // step,
        PER[0],
        [rows, rows],
        [edge, edge, cols(GROUP, 2 * tokens // POOL, width=step), cols(16, width=step)],
        [
            shape((2, BLOCK, width), BF16),
            shape((2, BLOCK, width), BF16),
            shape((GROUP, 2 * tokens // POOL, width), BF16),
            shape((16, width), BF16),
        ],
        "prepare",
    )(k, v)


def both(left, right):
    return jnp.concatenate([left, right], axis=1)


def near_scores(edge_ref, before, after, q):
    first = dot(before[0], q[:BLOCK], 1, 1) * LOG2 + edge_ref[0]
    return both(first, dot(after[0], q[BLOCK:], 1, 1) * LOG2 + edge_ref[1])


def join(stat_ref, acc_ref, s):
    own_top = stat_ref[0, 0:1]
    top = jnp.maximum(own_top, jnp.max(s, axis=0, keepdims=True))
    shrink = jnp.exp2(own_top - top)
    p = jnp.exp2(s - top)
    total = stat_ref[0, 1:2] * shrink + jnp.sum(p, axis=0, keepdims=True)
    return top, total, acc_ref[0] * shrink, p.astype(BF16)


def own_kernel(q_ref, k_ref, v_ref, acc_ref, stat_ref):
    s = dot(k_ref[...], q_ref[...], 1, 1) * LOG2
    top = jnp.max(s, axis=0, keepdims=True)
    p = jnp.exp2(s - top)
    stat_ref[0, 0:1] = top
    stat_ref[0, 1:2] = jnp.sum(p, axis=0, keepdims=True)
    acc_ref[0] = dot(v_ref[...], p.astype(BF16), 0, 0)


def forward_own(q, k, v):
    tokens, width = q.shape
    heads = width // HEAD
    rows = cols(tokens)
    return over_heads(
        own_kernel,
        heads,
        PER[1],
        [rows, rows, rows],
        [heads_of(HEAD, tokens), heads_of(2, tokens)],
        [shape((heads, HEAD, tokens), F32), shape((heads, 2, tokens), F32)],
        "forward_own",
    )(q, k, v)


def coarse_rows(one, two):
    half = one.shape[1] // 2
    middle = [one[:, which * half : (which + 1) * half].reshape(-1, HEAD) for which in range(2)]
    per_member = two.shape[1]
    count = GROUP * per_member
    pairs = one.shape[1] // (2 * POOL)
    groups = per_member // (2 * pairs)
    to = lax.broadcasted_iota(jnp.int32, (count, count), 0)
    at = lax.broadcasted_iota(jnp.int32, (count, count), 1)
    member = to // (groups * pairs) % GROUP
    source = member * per_member + to // pairs % groups * 2 * pairs + to // (count // 2) * pairs + to % pairs
    top = dot((at == source).astype(BF16), two[...].reshape(count, HEAD), 1, 0).astype(BF16)
    keys = jnp.concatenate([middle[0], top[: count // 2]], axis=0)
    values = jnp.concatenate([middle[1], top[count // 2 :]], axis=0)
    return keys, values


def forward_coarse_kernel(bias_ref, q_ref, one, two, acc_ref, stat_ref, out_ref, new_ref):
    keys, values = coarse_rows(one, two)
    s = dot(keys, q_ref[...], 1, 1) * LOG2 + bias_ref[...]
    top, total, out, p = join(stat_ref, acc_ref, s)
    new_ref[0, 0:1] = top
    new_ref[0, 1:2] = total
    out_ref[0] = out + dot(values, p, 0, 0)


def forward_coarse(bias, q, one, two, acc, stat):
    tokens, width = q.shape
    heads = width // HEAD
    state = [heads_of(HEAD, tokens), heads_of(2, tokens)]
    return over_heads(
        forward_coarse_kernel,
        heads,
        PER[3],
        [fixed(*bias.shape), cols(tokens), cols(*one.shape[:2]), cols(*two.shape[:2])] + state,
        state,
        [shape((heads, HEAD, tokens), F32), shape((heads, 2, tokens), F32)],
        "forward_coarse",
    )(bias, q, one, two, acc, stat)


def forward_near_kernel(
    edge_ref, q_ref, g_ref, before, after, acc_ref, own_ref, attn_ref, across_ref, stat_ref
):
    s = near_scores(edge_ref, before, after, q_ref[...])
    top, total, out, p = join(own_ref, acc_ref, s)
    out = out + both(dot(before[1], p[:, :BLOCK], 0, 0), dot(after[1], p[:, BLOCK:], 0, 0))
    across = (out / total).astype(BF16)
    across_ref[...] = across
    attn_ref[...] = jnp.transpose(across.astype(F32)).astype(BF16)
    stat_ref[0, 0:1] = top + jnp.log2(total)
    stat_ref[0, 1:2] = jnp.sum(jnp.transpose(g_ref[...].astype(F32)) * across.astype(F32), axis=0, keepdims=True)


def forward_near(edge, q, g, before, after, acc, stat):
    tokens, width = q.shape
    heads = width // HEAD
    rows = cols(tokens)
    near = cols(2, BLOCK)
    return over_heads(
        forward_near_kernel,
        heads,
        PER[2],
        [SMEM, rows, rows, near, near, heads_of(HEAD, tokens), heads_of(2, tokens)],
        [rows, leading(HEAD, tokens), heads_of(2, tokens)],
        [
            shape((tokens, width), BF16),
            shape((width, tokens), BF16),
            shape((heads, 2, tokens), F32),
        ],
        "forward_near",
    )(edge, q, g, before, after, acc, stat)


def weight_kernel(core_ref, across_ref, up_ref, keep_ref, send_ref):
    weight = dot(across_ref[...], up_ref[...], 1, 0).astype(BF16)
    first = core_ref[0] == 0
    keep_ref[0] = jnp.where(first, weight[:, :HEAD], weight[:, HEAD:])
    send_ref[0] = jnp.where(first, weight[:, HEAD:], weight[:, :HEAD])


def weight_terms(core, across, upstream):
    width, tokens = across.shape
    model = upstream.shape[1]
    pairs = model // (2 * HEAD)
    return over_heads(
        weight_kernel,
        pairs,
        PER[7],
        [SMEM, fixed(width, tokens), cols(tokens, width=2 * HEAD)],
        [leading(1, width, HEAD)] * 2,
        [shape((pairs, width, HEAD), BF16)] * 2,
        "weight_terms",
    )(core, across, upstream)


def gradients(s, dprob, stat_ref):
    p = jnp.exp2(s - stat_ref[0, 0:1])
    return p.astype(BF16), (p * (dprob - stat_ref[0, 1:2])).astype(BF16)


def backward_near_kernel(
    edge_ref, q_ref, g_ref, before, after, stat_ref, part_ref, sum_ref, dbefore_ref, dafter_ref
):
    q, g = q_ref[...], g_ref[...]
    s = near_scores(edge_ref, before, after, q)
    dprob = both(dot(before[1], g[:BLOCK], 1, 1), dot(after[1], g[BLOCK:], 1, 1))
    p, ds = gradients(s, dprob, stat_ref)
    for side, ref in enumerate((dbefore_ref, dafter_ref)):
        rows = slice(side * BLOCK, (side + 1) * BLOCK)
        ref[0] = (dot(ds[:, rows], q[rows], 1, 0) * FACTOR).astype(BF16)
        ref[1] = dot(p[:, rows], g[rows], 1, 0).astype(BF16)
    dq = both(dot(before[0], ds[:, :BLOCK], 0, 0), dot(after[0], ds[:, BLOCK:], 0, 0))
    sum_ref[0] = part_ref[0] + dq


def backward_near(edge, q, g, before, after, stat, part):
    tokens, width = q.shape
    heads = width // HEAD
    rows = cols(tokens)
    near = cols(2, BLOCK)
    return over_heads(
        backward_near_kernel,
        heads,
        PER[4],
        [SMEM, rows, rows, near, near, heads_of(2, tokens), heads_of(HEAD, tokens)],
        [heads_of(HEAD, tokens), near, near],
        [shape((heads, HEAD, tokens), F32), shape((2, BLOCK, width), BF16), shape((2, BLOCK, width), BF16)],
        "backward_near",
    )(edge, q, g, before, after, stat, part)


def backward_coarse_kernel(bias_ref, q_ref, g_ref, one, two, stat_ref, sum_ref, out_ref):
    q, g = q_ref[...], g_ref[...]
    keys, values = coarse_rows(one, two)
    s = dot(keys, q, 1, 1) * LOG2 + bias_ref[...]
    p, ds = gradients(s, dot(values, g, 1, 1), stat_ref)
    dk = dot(ds, q, 1, 0) * FACTOR
    dv = dot(p, g, 1, 0)
    sum_ref[0] = dot(keys, ds, 0, 0)
    count = one.shape[0] * (one.shape[1] // 2)
    pieces = [d.reshape(out_ref.shape[0], -1, HEAD) for d in (dk[:count], dv[:count], dk[count:], dv[count:])]
    out_ref[:, 0] = jnp.concatenate(pieces, axis=1).astype(BF16)


def backward_coarse(bias, q, g, one, two, stat):
    tokens, width = q.shape
    heads = width // HEAD
    rows = cols(tokens)
    slots, per_slot = one.shape[0], one.shape[1] + two.shape[1]
    return over_heads(
        backward_coarse_kernel,
        heads,
        PER[5],
        [
            fixed(*bias.shape), rows, rows, cols(*one.shape[:2]), cols(*two.shape[:2]), heads_of(2, tokens),
        ],
        [heads_of(HEAD, tokens), second(slots, 1, per_slot, HEAD)],
        [
            shape((heads, HEAD, tokens), F32),
            shape((slots, heads, per_slot, HEAD), BF16),
        ],
        "backward_coarse",
    )(bias, q, g, one, two, stat)


def backward_own_kernel(q_ref, k_ref, v_ref, g_ref, stat_ref, part_ref, dq_ref, down_ref):
    q, k, v, g = q_ref[...], k_ref[...], v_ref[...], g_ref[...]
    p, ds = gradients(dot(k, q, 1, 1) * LOG2, dot(v, g, 1, 1), stat_ref)
    down_ref[0] = dot(ds, q, 1, 0) * FACTOR
    down_ref[1] = dot(p, g, 1, 0)
    dq_ref[...] = jnp.transpose((part_ref[0] + dot(k, ds, 0, 0)) * FACTOR).astype(BF16)


def backward_own(q, k, v, g, stat, part):
    tokens, width = q.shape
    heads = width // HEAD
    rows = cols(tokens)
    return over_heads(
        backward_own_kernel,
        heads,
        PER[4],
        [rows, rows, rows, rows, heads_of(2, tokens), heads_of(HEAD, tokens)],
        [rows, cols(2, tokens)],
        [shape((tokens, width), BF16), shape((2, tokens, width), F32)],
        "backward_own",
    )(q, k, v, g, stat, part)


def project_kernel(attn_ref, weight_ref, out_ref):
    out_ref[...] = dot(attn_ref[...], weight_ref[...], 1, 0).astype(BF16)


def project(attn, weight):
    tokens, width = attn.shape
    model = weight.shape[1]
    step = 2 * HEAD
    return over_heads(
        project_kernel,
        model // step,
        1,
        [fixed(tokens, width), cols(width, width=step)],
        [cols(tokens, width=step)],
        [shape((tokens, model), BF16)],
        "project",
    )(attn, weight)[0]


def finish_kernel(own, first, last, coarse, two_ref, dk_ref, dv_ref):
    tokens = own.shape[1]
    size = tokens // POOL
    one = jnp.sum(coarse[:, : 2 * size].astype(F32), axis=0)
    for which, out_ref in enumerate((dk_ref, dv_ref)):
        term = one[which * size : (which + 1) * size] * SCALE
        term = jnp.broadcast_to(term[:, None], (size, POOL, HEAD)).reshape(tokens, HEAD)
        for side, edge in enumerate((first, last)):
            rows = slice(side * BLOCK, (side + 1) * BLOCK)
            at = 2 * which + side
            top = two_ref[0, at : at + 1] * (SCALE * SCALE)
            out_ref[rows, :] = (own[which, rows] + term[rows] + top + edge[which].astype(F32)).astype(BF16)


def finish(own, first, last, coarse, rows, two):
    tokens, width = own.shape[1:]
    heads = width // HEAD
    return over_heads(
        finish_kernel,
        heads,
        PER[6],
        [
            cols(2, tokens), cols(2, BLOCK), cols(2, BLOCK),
            second(coarse.shape[0], rows, HEAD), heads_of(*two.shape[1:]),
        ],
        [cols(tokens)] * 2,
        [shape((tokens, width), BF16)] * 2,
        "finish",
    )(own, first, last, coarse, two)


def exchange(x, axis, groups=None):
    return lax.all_to_all(x, axis, 0, 0, axis_index_groups=groups, tiled=True)


def masks(device, devices, tokens):
    group = device // GROUP
    per_group = GROUP * tokens // BLOCK
    block = device * (tokens // BLOCK) + jnp.arange(2, dtype=jnp.int32)[:, None]
    one = group * per_group + jnp.arange(GROUP * tokens // POOL, dtype=jnp.int32) * POOL // BLOCK
    pairs = tokens // BLOCK
    groups = devices // GROUP
    at = jnp.arange(devices * pairs, dtype=jnp.int32)
    two = (group - at // pairs) % groups * per_group + at // (pairs * groups) * pairs + at % pairs
    one_ok = jnp.abs(one[None] - block) > 1
    two_ok = (jnp.abs(two[None] - block) > 1) & (two // per_group != group)[None]
    ok = jnp.concatenate([one_ok, two_ok], axis=1)
    bias = jnp.where(ok, 0.0, MASKED).astype(F32)
    bias = jnp.repeat(bias.T, BLOCK, axis=1)
    edge = jnp.stack([device == 0, device == devices - 1]).astype(F32) * MASKED
    return edge, bias


def after_all(x, *others):
    return lax.optimization_barrier((x,) + others)[0]


def on_device(queries, keys, values, grad_out, out_weight):
    q, k, v, upstream = queries[0], keys[0], values[0], grad_out[0]
    tokens, width = q.shape
    model = upstream.shape[1]
    devices = lax.axis_size("ctx")
    dp = lax.axis_size("dp")
    device = lax.axis_index("ctx")
    groups = devices // GROUP
    near = [[g * GROUP + i for i in range(GROUP)] for g in range(groups)]
    up = [(i, i + 1) for i in range(devices - 1)]
    down = [(i + 1, i) for i in range(devices - 1)]
    rows_one = tokens // POOL

    pairs = tokens // BLOCK

    far = [[(i, (i + step * GROUP) % devices) for i in range(devices)] for step in range(groups)]
    back = [[(j, i) for i, j in moves] for moves in far]

    last, first, one, two = prepare(k, v)
    one = exchange(one, "ctx", near)
    two = [two] + [lax.ppermute(two, "ctx", moves) for moves in far[1:]]
    two = jnp.stack(two).reshape(groups, 2, -1, width)[:, :, :pairs].reshape(-1, width)
    two = jnp.broadcast_to(two[None], (GROUP,) + two.shape)
    edge, bias = masks(device, devices, tokens)
    acc, stat = forward_own(q, k, v)
    one = after_all(one, acc)
    two = after_all(two, one)
    two = exchange(two, "ctx", near)
    last, first = lax.optimization_barrier((last, first, two))[:2]
    g = dot(after_all(upstream, last), out_weight, 1, 1).astype(BF16)
    before = lax.ppermute(last, "ctx", up)
    after = lax.ppermute(first, "ctx", down)
    acc, stat = forward_coarse(bias, after_all(q, last, g), one, two, acc, stat)
    before, after = lax.optimization_barrier((before, after, acc))[:2]
    attn, across, stat = forward_near(edge, q, g, before, after, acc, stat)

    heads = width // HEAD
    part, packed = backward_coarse(bias, q, g, one, two, stat)
    packed = packed.reshape(GROUP, -1, HEAD)
    g, stat = lax.optimization_barrier((g, stat, packed))[:2]
    across = after_all(across, packed)
    packed = exchange(packed, "ctx", near)
    place = lax.axis_index("dp")
    core = (place % 2).reshape(1).astype(jnp.int32)
    keep, send = weight_terms(core, across, upstream)
    other = lax.ppermute(send, "dp", [(i, i ^ 1) for i in range(dp)])
    part, d_before, d_after = backward_near(edge, q, g, before, after, after_all(stat, send), part)
    other, packed = lax.optimization_barrier((other, packed, part))[:2]
    shares = []
    for step in range(dp // 2):
        at = (place // 2 + step) % (dp // 2)
        share = lax.dynamic_index_in_dim(keep, at, 0, False).astype(F32)
        share = share + lax.dynamic_index_in_dim(other, at, 0, False).astype(F32)
        shares.append(share.astype(BF16))
    sent = [
        lax.ppermute(share, "dp", [(i, (i + 2 * step) % dp) for i in range(dp)])
        for step, share in enumerate(shares)
        if step
    ]
    d_before, d_after = lax.optimization_barrier((d_before, d_after, packed, *shares))[:2]
    from_after = lax.ppermute(d_before, "ctx", down)
    from_before = lax.ppermute(d_after, "ctx", up)
    dq, d_own = backward_own(after_all(q, d_before), k, v, g, stat, part)
    sent = lax.optimization_barrier((dq, *sent))[1:]
    weight = sum((share.astype(F32) for share in sent), shares[0].astype(F32)).astype(BF16)
    weight = weight.reshape(groups, GROUP, -1, HEAD).transpose(1, 0, 2, 3).reshape(GROUP, -1, HEAD)
    mixed = project(after_all(attn, weight), out_weight)
    weight = exchange(weight, "ctx", near)
    weight = after_all(weight, from_after, from_before, mixed)
    weight = jnp.sum(weight.astype(F32), axis=0).astype(BF16).reshape(groups, -1, HEAD)
    d_two = packed.reshape(GROUP, heads, -1, HEAD)[:, :, 2 * rows_one :].astype(F32)
    d_two = jnp.sum(d_two, axis=0).astype(BF16).reshape(heads, 2, groups, pairs, HEAD)
    d_two = d_two.transpose(2, 0, 1, 3, 4).reshape(groups, -1, HEAD)
    count = d_two.shape[1]
    sums = []
    for step, moves in enumerate(back):
        at = (device // GROUP - step) % groups
        piece = jnp.concatenate([d_two[step], lax.dynamic_index_in_dim(weight, at, 0, False)], axis=0)
        sums.append(lax.ppermute(piece, "ctx", moves) if step else piece)
    sums = sum(piece.astype(F32) for piece in sums)
    mine_two = sums[:count].reshape(heads, 2 * pairs, HEAD)
    weight = sums[count:].astype(BF16)
    weight = exchange(jnp.broadcast_to(weight[None], (dp,) + weight.shape), "dp")
    grad_weight = jnp.swapaxes(weight, 0, 1).reshape(-1, model).astype(F32)

    grad_keys, grad_values = finish(d_own, from_before, from_after, packed, packed.shape[1] // heads, mine_two)
    return mixed[None], dq[None], grad_keys[None], grad_values[None], grad_weight


def solution(mesh):
    rows = P("dp", "ctx", None)
    return jax.shard_map(
        on_device,
        mesh=mesh,
        in_specs=(rows, rows, rows, rows, P()),
        out_specs=(rows, rows, rows, rows, P("ctx", None)),
        check_vma=False,
    )
```

```python
import math

import jax
import jax.numpy as jnp
from jax import lax
from jax.experimental import pallas as pl
from jax.experimental.pallas import tpu as pltpu
from jax.sharding import PartitionSpec as P

HEAD = 128
BLOCK = 256
POOL = 16
GROUP = 8
SCALE = 1.0 / math.sqrt(POOL)
FACTOR = 1.0 / math.sqrt(HEAD)
LOG2 = FACTOR * math.log2(math.e)
MASKED = -1e30
F32 = jnp.float32
BF16 = jnp.bfloat16
PER = (2, 2, 2, 2, 2, 2, 4, 2)
PARAMS = pltpu.CompilerParams(vmem_limit_bytes=56 * 1024 * 1024)


def dot(a, b, da, db):
    return lax.dot_general(a, b, (((da,), (db,)), ((), ())), preferred_element_type=F32)


def shape(dims, kind):
    return jax.ShapeDtypeStruct(dims, kind)


def cols(*lead, width=HEAD):
    def spec(per):
        return pl.BlockSpec(lead + (width * per,), lambda h: (0,) * len(lead) + (h,))

    return spec, lambda ref, i: ref.at[(slice(None),) * len(lead) + (pl.ds(i * width, width),)]


def heads_of(*dims):
    def spec(per):
        return pl.BlockSpec((per,) + dims, lambda h: (h,) + (0,) * len(dims))

    return spec, lambda ref, i: ref.at[pl.ds(i, 1)]


def second(lead, rows, *rest):
    def spec(per):
        return pl.BlockSpec((lead, rows * per) + rest, lambda h: (0, h) + (0,) * len(rest))

    return spec, lambda ref, i: ref.at[:, pl.ds(i * rows, rows)]


def leading(rows, *rest):
    def spec(per):
        return pl.BlockSpec((rows * per,) + rest, lambda h: (h,) + (0,) * len(rest))

    return spec, lambda ref, i: ref.at[pl.ds(i * rows, rows)]


def fixed(*dims):
    return lambda per: pl.BlockSpec(dims, lambda h: (0,) * len(dims)), lambda ref, i: ref


SMEM = lambda per: pl.BlockSpec(memory_space=pltpu.SMEM), lambda ref, i: ref


def over_heads(kernel, steps, per, ins, outs, out_shape, name, flops=1):
    def body(*refs):
        for i in range(per):
            kernel(*(view(ref, i) for ref, (_, view) in zip(refs, ins + outs)))

    return pl.pallas_call(
        body,
        grid=(steps // per,),
        in_specs=[spec(per) for spec, _ in ins],
        out_specs=[spec(per) for spec, _ in outs],
        out_shape=out_shape,
        compiler_params=PARAMS,
        cost_estimate=pl.CostEstimate(flops=flops, bytes_accessed=1, transcendentals=0),
        name=name,
    )


def pooling(count, rows):
    row = lax.broadcasted_iota(jnp.int32, (count, rows), 0)
    at = lax.broadcasted_iota(jnp.int32, (count, rows), 1)
    return (at // POOL == row).astype(BF16)


def prepare_kernel(k_ref, v_ref, last_ref, first_ref, one_ref, two_ref):
    tokens = k_ref.shape[0]
    count = tokens // POOL
    tops = []
    for which, ref in enumerate((k_ref, v_ref)):
        rows = ref[...]
        last_ref[which] = rows[tokens - BLOCK :]
        first_ref[which] = rows[:BLOCK]
        one = (dot(pooling(count, tokens), rows, 1, 0) * SCALE).astype(BF16)
        for slot in range(GROUP):
            one_ref[slot, which * count : (which + 1) * count] = one
        tops.append(dot(pooling(8, count), one, 1, 0) * SCALE)
    two_ref[...] = jnp.concatenate(tops, axis=0).astype(BF16)


def prepare(k, v):
    tokens, width = k.shape
    step = 2 * HEAD
    rows = cols(tokens, width=step)
    edge = cols(2, BLOCK, width=step)
    return over_heads(
        prepare_kernel,
        width // step,
        PER[0],
        [rows, rows],
        [edge, edge, cols(GROUP, 2 * tokens // POOL, width=step), cols(16, width=step)],
        [
            shape((2, BLOCK, width), BF16),
            shape((2, BLOCK, width), BF16),
            shape((GROUP, 2 * tokens // POOL, width), BF16),
            shape((16, width), BF16),
        ],
        "prepare",
    )(k, v)


def both(left, right):
    return jnp.concatenate([left, right], axis=1)


def near_scores(edge_ref, before, after, q):
    first = dot(before[0], q[:BLOCK], 1, 1) * LOG2 + edge_ref[0]
    return both(first, dot(after[0], q[BLOCK:], 1, 1) * LOG2 + edge_ref[1])


def join(stat_ref, acc_ref, s):
    own_top = stat_ref[0, 0:1]
    top = jnp.maximum(own_top, jnp.max(s, axis=0, keepdims=True))
    shrink = jnp.exp2(own_top - top)
    p = jnp.exp2(s - top)
    total = stat_ref[0, 1:2] * shrink + jnp.sum(p, axis=0, keepdims=True)
    return top, total, acc_ref[0] * shrink, p.astype(BF16)


def own_kernel(q_ref, k_ref, v_ref, acc_ref, stat_ref):
    s = dot(k_ref[...], q_ref[...], 1, 1) * LOG2
    top = jnp.max(s, axis=0, keepdims=True)
    p = jnp.exp2(s - top)
    stat_ref[0, 0:1] = top
    stat_ref[0, 1:2] = jnp.sum(p, axis=0, keepdims=True)
    acc_ref[0] = dot(v_ref[...], p.astype(BF16), 0, 0)


def forward_own(q, k, v):
    tokens, width = q.shape
    heads = width // HEAD
    rows = cols(tokens)
    return over_heads(
        own_kernel,
        heads,
        PER[1],
        [rows, rows, rows],
        [heads_of(HEAD, tokens), heads_of(2, tokens)],
        [shape((heads, HEAD, tokens), F32), shape((heads, 2, tokens), F32)],
        "forward_own",
    )(q, k, v)


def coarse_rows(one, two):
    half = one.shape[1] // 2
    middle = [one[:, which * half : (which + 1) * half].reshape(-1, HEAD) for which in range(2)]
    per_member = two.shape[1]
    count = GROUP * per_member
    pairs = one.shape[1] // (2 * POOL)
    groups = per_member // (2 * pairs)
    to = lax.broadcasted_iota(jnp.int32, (count, count), 0)
    at = lax.broadcasted_iota(jnp.int32, (count, count), 1)
    member = to // (groups * pairs) % GROUP
    source = member * per_member + to // pairs % groups * 2 * pairs + to // (count // 2) * pairs + to % pairs
    top = dot((at == source).astype(BF16), two[...].reshape(count, HEAD), 1, 0).astype(BF16)
    keys = jnp.concatenate([middle[0], top[: count // 2]], axis=0)
    values = jnp.concatenate([middle[1], top[count // 2 :]], axis=0)
    return keys, values


def forward_coarse_kernel(bias_ref, q_ref, one, two, acc_ref, stat_ref, out_ref, new_ref):
    keys, values = coarse_rows(one, two)
    s = dot(keys, q_ref[...], 1, 1) * LOG2 + bias_ref[...]
    top, total, out, p = join(stat_ref, acc_ref, s)
    new_ref[0, 0:1] = top
    new_ref[0, 1:2] = total
    out_ref[0] = out + dot(values, p, 0, 0)


def forward_coarse(bias, q, one, two, acc, stat):
    tokens, width = q.shape
    heads = width // HEAD
    state = [heads_of(HEAD, tokens), heads_of(2, tokens)]
    return over_heads(
        forward_coarse_kernel,
        heads,
        PER[3],
        [fixed(*bias.shape), cols(tokens), cols(*one.shape[:2]), cols(*two.shape[:2])] + state,
        state,
        [shape((heads, HEAD, tokens), F32), shape((heads, 2, tokens), F32)],
        "forward_coarse",
    )(bias, q, one, two, acc, stat)


def forward_near_kernel(
    edge_ref, q_ref, g_ref, before, after, acc_ref, own_ref, attn_ref, across_ref, stat_ref
):
    s = near_scores(edge_ref, before, after, q_ref[...])
    top, total, out, p = join(own_ref, acc_ref, s)
    out = out + both(dot(before[1], p[:, :BLOCK], 0, 0), dot(after[1], p[:, BLOCK:], 0, 0))
    across = (out / total).astype(BF16)
    across_ref[...] = across
    attn_ref[...] = jnp.transpose(across.astype(F32)).astype(BF16)
    stat_ref[0, 0:1] = top + jnp.log2(total)
    stat_ref[0, 1:2] = jnp.sum(jnp.transpose(g_ref[...].astype(F32)) * across.astype(F32), axis=0, keepdims=True)


def weight_kernel(core_ref, across_ref, up_ref, keep_ref, send_ref):
    weight = dot(across_ref[...], up_ref[...], 1, 0).astype(BF16)
    first = core_ref[0] == 0
    keep_ref[0] = jnp.where(first, weight[:, :HEAD], weight[:, HEAD:])
    send_ref[0] = jnp.where(first, weight[:, HEAD:], weight[:, :HEAD])


def weight_terms(core, across, upstream):
    width, tokens = across.shape
    model = upstream.shape[1]
    pairs = model // (2 * HEAD)
    return over_heads(
        weight_kernel,
        pairs,
        PER[7],
        [SMEM, fixed(width, tokens), cols(tokens, width=2 * HEAD)],
        [leading(1, width, HEAD)] * 2,
        [shape((pairs, width, HEAD), BF16)] * 2,
        "weight_terms",
    )(core, across, upstream)


def gradients(s, dprob, stat_ref):
    p = jnp.exp2(s - stat_ref[0, 0:1])
    return p.astype(BF16), (p * (dprob - stat_ref[0, 1:2])).astype(BF16)


def backward_near_kernel(
    edge_ref, q_ref, g_ref, before, after, stat_ref, part_ref, sum_ref, dbefore_ref, dafter_ref
):
    q, g = q_ref[...], g_ref[...]
    s = near_scores(edge_ref, before, after, q)
    dprob = both(dot(before[1], g[:BLOCK], 1, 1), dot(after[1], g[BLOCK:], 1, 1))
    p, ds = gradients(s, dprob, stat_ref)
    for side, ref in enumerate((dbefore_ref, dafter_ref)):
        rows = slice(side * BLOCK, (side + 1) * BLOCK)
        ref[0] = (dot(ds[:, rows], q[rows], 1, 0) * FACTOR).astype(BF16)
        ref[1] = dot(p[:, rows], g[rows], 1, 0).astype(BF16)
    dq = both(dot(before[0], ds[:, :BLOCK], 0, 0), dot(after[0], ds[:, BLOCK:], 0, 0))
    sum_ref[0] = part_ref[0] + dq


def backward_near(edge, q, g, before, after, stat, part):
    tokens, width = q.shape
    heads = width // HEAD
    rows = cols(tokens)
    near = cols(2, BLOCK)
    return over_heads(
        backward_near_kernel,
        heads,
        PER[4],
        [SMEM, rows, rows, near, near, heads_of(2, tokens), heads_of(HEAD, tokens)],
        [heads_of(HEAD, tokens), near, near],
        [shape((heads, HEAD, tokens), F32), shape((2, BLOCK, width), BF16), shape((2, BLOCK, width), BF16)],
        "backward_near",
    )(edge, q, g, before, after, stat, part)


def backward_coarse_kernel(bias_ref, q_ref, g_ref, one, two, stat_ref, sum_ref, out_ref):
    q, g = q_ref[...], g_ref[...]
    keys, values = coarse_rows(one, two)
    s = dot(keys, q, 1, 1) * LOG2 + bias_ref[...]
    p, ds = gradients(s, dot(values, g, 1, 1), stat_ref)
    dk = dot(ds, q, 1, 0) * FACTOR
    dv = dot(p, g, 1, 0)
    sum_ref[0] = dot(keys, ds, 0, 0)
    count = one.shape[0] * (one.shape[1] // 2)
    pieces = [d.reshape(out_ref.shape[0], -1, HEAD) for d in (dk[:count], dv[:count], dk[count:], dv[count:])]
    out_ref[:, 0] = jnp.concatenate(pieces, axis=1).astype(BF16)


def middle_kernel(
    edge_ref, bias_ref, q_ref, g_ref, before, after, one, two, acc_ref, own_ref,
    attn_ref, across_ref, stat_ref, sum_ref, out_ref,
):
    forward_near_kernel(edge_ref, q_ref, g_ref, before, after, acc_ref, own_ref, attn_ref, across_ref, stat_ref)
    backward_coarse_kernel(bias_ref, q_ref, g_ref, one, two, stat_ref, sum_ref, out_ref)


def middle(edge, bias, q, g, before, after, one, two, acc, stat):
    tokens, width = q.shape
    heads = width // HEAD
    rows = cols(tokens)
    near = cols(2, BLOCK)
    slots, per_slot = one.shape[0], one.shape[1] + two.shape[1]
    return over_heads(
        middle_kernel,
        heads,
        PER[2],
        [
            SMEM, fixed(*bias.shape), rows, rows, near, near, cols(*one.shape[:2]), cols(*two.shape[:2]),
            heads_of(HEAD, tokens), heads_of(2, tokens),
        ],
        [
            rows, leading(HEAD, tokens), heads_of(2, tokens), heads_of(HEAD, tokens),
            second(slots, 1, per_slot, HEAD),
        ],
        [
            shape((tokens, width), BF16),
            shape((width, tokens), BF16),
            shape((heads, 2, tokens), F32),
            shape((heads, HEAD, tokens), F32),
            shape((slots, heads, per_slot, HEAD), BF16),
        ],
        "middle",
    )(edge, bias, q, g, before, after, one, two, acc, stat)


def backward_near_kernel(
    edge_ref, q_ref, g_ref, before, after, stat_ref, part_ref, sum_ref, dbefore_ref, dafter_ref
):
    q, g = q_ref[...], g_ref[...]
    s = near_scores(edge_ref, before, after, q)
    dprob = both(dot(before[1], g[:BLOCK], 1, 1), dot(after[1], g[BLOCK:], 1, 1))
    p, ds = gradients(s, dprob, stat_ref)
    for side, ref in enumerate((dbefore_ref, dafter_ref)):
        rows = slice(side * BLOCK, (side + 1) * BLOCK)
        ref[0] = (dot(ds[:, rows], q[rows], 1, 0) * FACTOR).astype(BF16)
        ref[1] = dot(p[:, rows], g[rows], 1, 0).astype(BF16)
    dq = both(dot(before[0], ds[:, :BLOCK], 0, 0), dot(after[0], ds[:, BLOCK:], 0, 0))
    sum_ref[0] = part_ref[0] + dq


def backward_near(edge, q, g, before, after, stat, part):
    tokens, width = q.shape
    heads = width // HEAD
    rows = cols(tokens)
    near = cols(2, BLOCK)
    return over_heads(
        backward_near_kernel,
        heads,
        PER[4],
        [SMEM, rows, rows, near, near, heads_of(2, tokens), heads_of(HEAD, tokens)],
        [heads_of(HEAD, tokens), near, near],
        [shape((heads, HEAD, tokens), F32), shape((2, BLOCK, width), BF16), shape((2, BLOCK, width), BF16)],
        "backward_near",
    )(edge, q, g, before, after, stat, part)


def backward_coarse_kernel(bias_ref, q_ref, g_ref, one, two, stat_ref, sum_ref, out_ref):
    q, g = q_ref[...], g_ref[...]
    keys, values = coarse_rows(one, two)
    s = dot(keys, q, 1, 1) * LOG2 + bias_ref[...]
    p, ds = gradients(s, dot(values, g, 1, 1), stat_ref)
    dk = dot(ds, q, 1, 0) * FACTOR
    dv = dot(p, g, 1, 0)
    sum_ref[0] = dot(keys, ds, 0, 0)
    count = one.shape[0] * (one.shape[1] // 2)
    pieces = [d.reshape(out_ref.shape[0], -1, HEAD) for d in (dk[:count], dv[:count], dk[count:], dv[count:])]
    out_ref[:, 0] = jnp.concatenate(pieces, axis=1).astype(BF16)


def backward_coarse(bias, q, g, one, two, stat):
    tokens, width = q.shape
    heads = width // HEAD
    rows = cols(tokens)
    slots, per_slot = one.shape[0], one.shape[1] + two.shape[1]
    return over_heads(
        backward_coarse_kernel,
        heads,
        PER[5],
        [
            fixed(*bias.shape), rows, rows, cols(*one.shape[:2]), cols(*two.shape[:2]), heads_of(2, tokens),
        ],
        [heads_of(HEAD, tokens), second(slots, 1, per_slot, HEAD)],
        [
            shape((heads, HEAD, tokens), F32),
            shape((slots, heads, per_slot, HEAD), BF16),
        ],
        "backward_coarse",
    )(bias, q, g, one, two, stat)


def backward_own_kernel(q_ref, k_ref, v_ref, g_ref, stat_ref, part_ref, dq_ref, down_ref):
    q, k, v, g = q_ref[...], k_ref[...], v_ref[...], g_ref[...]
    p, ds = gradients(dot(k, q, 1, 1) * LOG2, dot(v, g, 1, 1), stat_ref)
    down_ref[0] = dot(ds, q, 1, 0) * FACTOR
    down_ref[1] = dot(p, g, 1, 0)
    dq_ref[...] = jnp.transpose((part_ref[0] + dot(k, ds, 0, 0)) * FACTOR).astype(BF16)


def backward_own(q, k, v, g, stat, part):
    tokens, width = q.shape
    heads = width // HEAD
    rows = cols(tokens)
    return over_heads(
        backward_own_kernel,
        heads,
        PER[4],
        [rows, rows, rows, rows, heads_of(2, tokens), heads_of(HEAD, tokens)],
        [rows, cols(2, tokens)],
        [shape((tokens, width), BF16), shape((2, tokens, width), F32)],
        "backward_own",
    )(q, k, v, g, stat, part)


def project_kernel(attn_ref, weight_ref, out_ref):
    out_ref[...] = dot(attn_ref[...], weight_ref[...], 1, 0).astype(BF16)


def project(attn, weight):
    tokens, width = attn.shape
    model = weight.shape[1]
    step = 2 * HEAD
    return over_heads(
        project_kernel,
        model // step,
        1,
        [fixed(tokens, width), cols(width, width=step)],
        [cols(tokens, width=step)],
        [shape((tokens, model), BF16)],
        "project",
    )(attn, weight)[0]


def finish_kernel(own, first, last, coarse, two_ref, dk_ref, dv_ref):
    tokens = own.shape[1]
    size = tokens // POOL
    one = jnp.sum(coarse[:, : 2 * size].astype(F32), axis=0)
    for which, out_ref in enumerate((dk_ref, dv_ref)):
        term = one[which * size : (which + 1) * size] * SCALE
        term = jnp.broadcast_to(term[:, None], (size, POOL, HEAD)).reshape(tokens, HEAD)
        for side, edge in enumerate((first, last)):
            rows = slice(side * BLOCK, (side + 1) * BLOCK)
            at = 2 * which + side
            top = two_ref[0, at : at + 1] * (SCALE * SCALE)
            out_ref[rows, :] = (own[which, rows] + term[rows] + top + edge[which].astype(F32)).astype(BF16)


def finish(own, first, last, coarse, rows, two):
    tokens, width = own.shape[1:]
    heads = width // HEAD
    return over_heads(
        finish_kernel,
        heads,
        PER[6],
        [
            cols(2, tokens), cols(2, BLOCK), cols(2, BLOCK),
            second(coarse.shape[0], rows, HEAD), heads_of(*two.shape[1:]),
        ],
        [cols(tokens)] * 2,
        [shape((tokens, width), BF16)] * 2,
        "finish",
    )(own, first, last, coarse, two)


def exchange(x, axis, groups=None):
    return lax.all_to_all(x, axis, 0, 0, axis_index_groups=groups, tiled=True)


def masks(device, devices, tokens):
    group = device // GROUP
    per_group = GROUP * tokens // BLOCK
    block = device * (tokens // BLOCK) + jnp.arange(2, dtype=jnp.int32)[:, None]
    one = group * per_group + jnp.arange(GROUP * tokens // POOL, dtype=jnp.int32) * POOL // BLOCK
    pairs = tokens // BLOCK
    groups = devices // GROUP
    at = jnp.arange(devices * pairs, dtype=jnp.int32)
    two = (group - at // pairs) % groups * per_group + at // (pairs * groups) * pairs + at % pairs
    one_ok = jnp.abs(one[None] - block) > 1
    two_ok = (jnp.abs(two[None] - block) > 1) & (two // per_group != group)[None]
    ok = jnp.concatenate([one_ok, two_ok], axis=1)
    bias = jnp.where(ok, 0.0, MASKED).astype(F32)
    bias = jnp.repeat(bias.T, BLOCK, axis=1)
    edge = jnp.stack([device == 0, device == devices - 1]).astype(F32) * MASKED
    return edge, bias


def after_all(x, *others):
    return lax.optimization_barrier((x,) + others)[0]


def on_device(queries, keys, values, grad_out, out_weight):
    q, k, v, upstream = queries[0], keys[0], values[0], grad_out[0]
    tokens, width = q.shape
    model = upstream.shape[1]
    devices = lax.axis_size("ctx")
    dp = lax.axis_size("dp")
    device = lax.axis_index("ctx")
    groups = devices // GROUP
    near = [[g * GROUP + i for i in range(GROUP)] for g in range(groups)]
    up = [(i, i + 1) for i in range(devices - 1)]
    down = [(i + 1, i) for i in range(devices - 1)]
    rows_one = tokens // POOL

    pairs = tokens // BLOCK

    far = [[(i, (i + step * GROUP) % devices) for i in range(devices)] for step in range(groups)]
    back = [[(j, i) for i, j in moves] for moves in far]

    last, first, one, two = prepare(k, v)
    one = exchange(one, "ctx", near)
    two = [two] + [lax.ppermute(two, "ctx", moves) for moves in far[1:]]
    two = jnp.stack(two).reshape(groups, 2, -1, width)[:, :, :pairs].reshape(-1, width)
    two = jnp.broadcast_to(two[None], (GROUP,) + two.shape)
    edge, bias = masks(device, devices, tokens)
    acc, stat = forward_own(q, k, v)
    one = after_all(one, acc)
    two = after_all(two, one)
    two = exchange(two, "ctx", near)
    last, first = lax.optimization_barrier((last, first, two))[:2]
    g = dot(after_all(upstream, last), out_weight, 1, 1).astype(BF16)
    before = lax.ppermute(last, "ctx", up)
    after = lax.ppermute(first, "ctx", down)
    acc, stat = forward_coarse(bias, after_all(q, last, g), one, two, acc, stat)
    before, after = lax.optimization_barrier((before, after, acc))[:2]
    attn, across, stat, part, packed = middle(edge, bias, q, g, before, after, one, two, acc, stat)

    heads = width // HEAD
    packed = packed.reshape(GROUP, -1, HEAD)
    g, stat = lax.optimization_barrier((g, stat, packed))[:2]
    across = after_all(across, packed)
    packed = exchange(packed, "ctx", near)
    place = lax.axis_index("dp")
    core = (place % 2).reshape(1).astype(jnp.int32)
    keep, send = weight_terms(core, across, upstream)
    other = lax.ppermute(send, "dp", [(i, i ^ 1) for i in range(dp)])
    part, d_before, d_after = backward_near(edge, q, g, before, after, after_all(stat, send), part)
    other, packed = lax.optimization_barrier((other, packed, part))[:2]
    shares = []
    for step in range(dp // 2):
        at = (place // 2 + step) % (dp // 2)
        share = lax.dynamic_index_in_dim(keep, at, 0, False).astype(F32)
        share = share + lax.dynamic_index_in_dim(other, at, 0, False).astype(F32)
        shares.append(share.astype(BF16))
    sent = [
        lax.ppermute(share, "dp", [(i, (i + 2 * step) % dp) for i in range(dp)])
        for step, share in enumerate(shares)
        if step
    ]
    d_before, d_after = lax.optimization_barrier((d_before, d_after, packed, *shares))[:2]
    from_after = lax.ppermute(d_before, "ctx", down)
    from_before = lax.ppermute(d_after, "ctx", up)
    dq, d_own = backward_own(after_all(q, d_before), k, v, g, stat, part)
    sent = lax.optimization_barrier((dq, *sent))[1:]
    weight = sum((share.astype(F32) for share in sent), shares[0].astype(F32)).astype(BF16)
    weight = weight.reshape(groups, GROUP, -1, HEAD).transpose(1, 0, 2, 3).reshape(GROUP, -1, HEAD)
    mixed = project(after_all(attn, weight), out_weight)
    weight = exchange(weight, "ctx", near)
    weight = after_all(weight, from_after, from_before, mixed)
    weight = jnp.sum(weight.astype(F32), axis=0).astype(BF16).reshape(groups, -1, HEAD)
    d_two = packed.reshape(GROUP, heads, -1, HEAD)[:, :, 2 * rows_one :].astype(F32)
    d_two = jnp.sum(d_two, axis=0).astype(BF16).reshape(heads, 2, groups, pairs, HEAD)
    d_two = d_two.transpose(2, 0, 1, 3, 4).reshape(groups, -1, HEAD)
    count = d_two.shape[1]
    sums = []
    for step, moves in enumerate(back):
        at = (device // GROUP - step) % groups
        piece = jnp.concatenate([d_two[step], lax.dynamic_index_in_dim(weight, at, 0, False)], axis=0)
        sums.append(lax.ppermute(piece, "ctx", moves) if step else piece)
    sums = sum(piece.astype(F32) for piece in sums)
    mine_two = sums[:count].reshape(heads, 2 * pairs, HEAD)
    weight = sums[count:].astype(BF16)
    weight = exchange(jnp.broadcast_to(weight[None], (dp,) + weight.shape), "dp")
    grad_weight = jnp.swapaxes(weight, 0, 1).reshape(-1, model).astype(F32)

    grad_keys, grad_values = finish(d_own, from_before, from_after, packed, packed.shape[1] // heads, mine_two)
    return mixed[None], dq[None], grad_keys[None], grad_values[None], grad_weight


def solution(mesh):
    rows = P("dp", "ctx", None)
    return jax.shard_map(
        on_device,
        mesh=mesh,
        in_specs=(rows, rows, rows, rows, P()),
        out_specs=(rows, rows, rows, rows, P("ctx", None)),
        check_vma=False,
    )
```
